512 devices in a mesh: grp: 4 (over y_hi, core), dev: 32 (over x, z), split: 4 (over y_lo).
Axes of the slice: x: 4, y: 8 (y_hi: 2, y_lo: 4; y = y_hi * 4 + y_lo), z: 8, core: 2. Of those that a mesh axis runs over, the one named last changes fastest.
Arguments:
- tokens: bfloat16 [16384, 2048], P(('grp', 'dev'), 'split'), may hold values from -6 to 6
- upstream: bfloat16 [16384, 2048], P(('grp', 'dev'), 'split'), may hold values from -0.29882812 to 0.29882812
- expert_ids: int32 [16384, 8], P(('grp', 'dev')), may hold values from 0 to 127, as said below
- gate_probs: float32 [16384, 8], P(('grp', 'dev')), may hold values from 0.1 to 0.5
- w_gate: bfloat16 [128, 2048, 768], P(('grp', 'dev'), None, 'split'), may hold values from -0.125 to 0.125
- w_up: bfloat16 [128, 2048, 768], P(('grp', 'dev'), None, 'split'), may hold values from -0.125 to 0.125
- w_down: bfloat16 [128, 768, 2048], P(('grp', 'dev'), None, 'split'), may hold values from -0.21875 to 0.21875
Outputs:
- mixed: bfloat16 [16384, 2048], P(('grp', 'dev'), 'split')
- gate_grads: float32 [16384, 8], P(('grp', 'dev'))
- down_grads: float32 [128, 768, 2048], P(('grp', 'dev'), None, 'split')
The draws below stay inside these ranges and needn't reach their ends.
Inputs may be any that keep to these rules, and one draw needn't show every extreme that they name: `expert_ids`: each row names 8 different experts. The 128 rows of one device name any one expert at most 16 times, and 4 experts, the same for every device, exactly 16 times on every device.
All inputs are finite; a program needn't handle non-finite values.
Results may differ from the reference program's by a relative error of at most 0.0058.
Values may be sent and summed in bfloat16 or wider, within the bound.
No kernel may reach another device: no remote copies, remote signals or barrier semaphores. Data moves between devices by JAX's collectives and lax.ppermute only.
A program may use at most 64 MiB of HBM per device.

```python
import jax
import jax.numpy as jnp
from jax import lax

D = 2048
FF = 768
TOP = 8
HOT = 4
TOK_DEV = 128
EXPERTS = 128
TOKENS = 16384
CAP = 16
N_GRP = 4
N_DEV = 32


def draw_expert_ids(key, part):
    blocks = TOKENS // TOK_DEV
    cold_count = EXPERTS - HOT
    base = jax.random.permutation(jax.random.fold_in(key, 11), EXPERTS).astype(jnp.int32)
    hot_ids = base[:HOT]
    cold_base = base[HOT:]
    block_keys = jax.random.split(jax.random.fold_in(key, 12), blocks)
    cold_order = jax.vmap(lambda one_key: jax.random.permutation(one_key, cold_count))(block_keys).astype(jnp.int32)
    cold_lists = cold_base[cold_order]
    shifts = jax.random.randint(jax.random.fold_in(key, 13), (blocks, HOT), 0, TOK_DEV).astype(jnp.int32)
    row_index = jnp.arange(TOK_DEV, dtype=jnp.int32)
    slot_index = jnp.arange(TOP, dtype=jnp.int32)
    position = (row_index[:, None] * TOP + slot_index[None, :]) % cold_count
    cold_ids = cold_lists[:, position]
    has_hot = (row_index[None, :, None] + shifts[:, None, :]) % TOK_DEV < CAP
    has_full = jnp.concatenate([has_hot, jnp.zeros((blocks, TOK_DEV, TOP - HOT), dtype=bool)], axis=2)
    hot_full = jnp.concatenate([hot_ids, jnp.zeros((TOP - HOT,), jnp.int32)])
    chosen = jnp.where(has_full, hot_full[None, None, :], cold_ids)
    return chosen.reshape(TOKENS, TOP).astype(jnp.int32)


def shard_levels(stream_key, shape, cuts, smallest, largest):
    level = 1.0
    for dim, blocks in cuts:
        draws = jax.random.uniform(jax.random.fold_in(jax.random.fold_in(stream_key, 6), dim), (blocks,), jnp.float32, smallest / len(cuts), largest / len(cuts))
        level = level * jnp.repeat(jnp.exp(draws), shape[dim] // blocks).reshape((-1,) + (1,) * (len(shape) - 1 - dim))
    return level


def centred(key, dims, scale, most, cuts=(), kind=jnp.bfloat16):
    array = jax.random.normal(key, dims, jnp.float32) * scale
    if len(cuts) > 0:
        array = shard_levels(key, dims, cuts, -0.22, 0.18) * array
    return jnp.clip(array, min=-most, max=most).astype(kind)


def setup_inputs(seed: int = 0) -> dict:
    key_list = jax.random.split(jax.random.key(seed), 8)
    return {
        "tokens": centred(key_list[0], (TOKENS, D), 1.0, 6.0, ((0, 128), (1, 4))),
        "upstream": centred(key_list[1], (TOKENS, D), 0.05, 0.29882812, ((0, 128), (1, 4))),
        "expert_ids": draw_expert_ids(jax.random.fold_in(key_list[7], 71), 0),
        "gate_probs": jnp.clip(0.1 + 0.4 * jax.random.uniform(key_list[3], (TOKENS, TOP), jnp.float32) ** shard_levels(key_list[3], (TOKENS, TOP), ((0, 128),), -0.2, 0.2), 0.1, 0.5),
        "w_gate": centred(key_list[4], (EXPERTS, D, FF), D ** -0.5, 0.125, ((0, 128), (2, 4))),
        "w_up": centred(key_list[5], (EXPERTS, D, FF), D ** -0.5, 0.125, ((0, 128), (2, 4))),
        "w_down": centred(key_list[6], (EXPERTS, FF, D), FF ** -0.5, 0.21875, ((0, 128), (2, 4))),
    }


def reference(tokens, upstream, expert_ids, gate_probs, w_gate, w_up, w_down):
    pair_count = TOKENS * TOP
    buffer_rows = N_GRP * N_DEV * CAP
    flat_ids = expert_ids.reshape(-1).astype(jnp.int32)
    order = jnp.argsort(flat_ids, stable=True).astype(jnp.int32)
    table = (flat_ids[:, None] == jnp.arange(EXPERTS, dtype=jnp.int32)[None, :]).astype(jnp.int32)
    counts = jnp.sum(table, axis=0).astype(jnp.int32)
    starts = (jnp.cumsum(counts) - counts).astype(jnp.int32)
    padded_order = jnp.concatenate([order, jnp.zeros((buffer_rows,), jnp.int32)])
    flat_gates = gate_probs.reshape(-1)

    def one_expert(index):
        chosen = lax.dynamic_slice_in_dim(padded_order, starts[index].astype(jnp.int32), buffer_rows, 0)
        valid = jnp.arange(buffer_rows, dtype=jnp.int32) < counts[index]
        token_rows = chosen // TOP
        inputs = jnp.where(valid[:, None], tokens[token_rows], jnp.zeros((), tokens.dtype))
        pre_gate = jnp.dot(inputs, w_gate[index], preferred_element_type=jnp.float32)
        pre_up = jnp.dot(inputs, w_up[index], preferred_element_type=jnp.float32)
        hidden = (jax.nn.silu(pre_gate) * pre_up).astype(jnp.bfloat16)
        outputs = jnp.dot(hidden, w_down[index], preferred_element_type=jnp.float32).astype(jnp.bfloat16)
        weights = jnp.where(valid, flat_gates[chosen], jnp.zeros((), flat_gates.dtype))
        scaled = (weights[:, None] * upstream[token_rows].astype(jnp.float32)).astype(jnp.bfloat16)
        grad = jnp.dot(hidden.T, scaled, preferred_element_type=jnp.float32)
        return outputs, grad

    outputs, down_grads = lax.map(one_expert, jnp.arange(EXPERTS, dtype=jnp.int32))
    rank = jnp.zeros((pair_count,), jnp.int32).at[order].set(jnp.arange(pair_count, dtype=jnp.int32))
    place = flat_ids * buffer_rows + rank - starts[flat_ids]
    pair_out = outputs.reshape(EXPERTS * buffer_rows, D)[place].reshape(TOKENS, TOP, D)
    pair_wide = pair_out.astype(jnp.float32)
    mixed = jnp.einsum("tk,tkd->td", gate_probs.astype(jnp.float32), pair_wide).astype(jnp.bfloat16)
    gate_grads = jnp.einsum("td,tkd->tk", upstream.astype(jnp.float32), pair_wide)
    return mixed, gate_grads, down_grads
```

```python
import jax
import jax.numpy as jnp
from jax import lax
from jax.sharding import PartitionSpec as P

SLOTS = 16


def bf16_pieces(x, count):
    pieces = []
    for _ in range(count):
        top = lax.reduce_precision(x, exponent_bits=8, mantissa_bits=7)
        pieces.append(top.astype(jnp.bfloat16))
        x = x - top
    return pieces


def per_device(tokens, upstream, expert_ids, gate_probs, w_gate, w_up, w_down):
    grp = lax.axis_size("grp")
    dev = lax.axis_size("dev")
    split = lax.axis_size("split")
    grp_me = lax.axis_index("grp")
    split_me = lax.axis_index("split")
    rows, top = expert_ids.shape
    feats = tokens.shape[1]
    hidden_part = w_gate.shape[2]
    f32, bf16 = jnp.float32, jnp.bfloat16

    w_own = jnp.concatenate([w_gate[0].T, w_up[0].T], axis=0)
    w_all = lax.all_gather(w_own, "split", axis=0, tiled=False)

    ids_t = expert_ids.T.astype(bf16)
    meta = jnp.concatenate([ids_t] + bf16_pieces(gate_probs.T, 3), axis=0)
    meta = meta.reshape(-1, 2 * feats)
    meta = jnp.pad(meta, ((0, SLOTS - meta.shape[0]), (0, 0)))
    both = jnp.concatenate([jnp.concatenate([tokens, upstream], axis=1), meta], axis=0)
    both = jnp.broadcast_to(both[None], (grp,) + both.shape)
    near = lax.all_to_all(both, "grp", split_axis=0, concat_axis=0, tiled=True)
    near_tokens = near[:, :rows, :feats]
    near_upstream = near[:, :rows, feats:]
    near_meta = near[:, rows : rows + 4 * top * rows // (2 * feats), :].reshape(grp, 4, top, rows).astype(f32)
    near_ids = near_meta[:, 0]
    near_gates = near_meta[:, 1] + near_meta[:, 2] + near_meta[:, 3]

    mine = lax.all_to_all(near_tokens, "split", split_axis=0, concat_axis=0, tiled=True)
    mine = jnp.concatenate([mine[i] for i in range(split)], axis=1)

    expert = (grp_me * dev).astype(f32) + lax.broadcasted_iota(f32, (1, dev, 1), 1)
    equal = [near_ids[:, k][:, None, :] == expert for k in range(top)]
    member = sum(e.astype(f32) for e in equal)
    gate_of = sum(jnp.where(e, near_gates[:, k][:, None, :], 0.0) for k, e in enumerate(equal))
    before = (
        lax.broadcasted_iota(jnp.int32, (rows, rows), 0) < lax.broadcasted_iota(jnp.int32, (rows, rows), 1)
    ).astype(bf16)
    place = jnp.dot(member.astype(bf16).reshape(grp * dev, rows), before, preferred_element_type=f32)
    place = jnp.where(member > 0, place.reshape(grp, dev, rows), -1.0)
    slot = lax.broadcasted_iota(f32, (1, 1, SLOTS, 1), 2)
    chosen = place[:, :, None, :] == slot
    pick = chosen.astype(bf16).reshape(grp, dev * SLOTS, rows)
    weight = jnp.where(chosen, gate_of[:, :, None, :], 0.0).reshape(grp, dev * SLOTS, rows)
    gate_row = jnp.sum(weight, axis=2, keepdims=True)

    pick_mine = lax.dynamic_index_in_dim(pick, split_me, 0, keepdims=False)
    send = jnp.dot(pick_mine, mine, preferred_element_type=f32).astype(bf16)
    arrived = lax.all_to_all(
        send.reshape(dev, SLOTS, split * feats), "dev", split_axis=0, concat_axis=0, tiled=True
    ).reshape(dev * SLOTS, split * feats)
    scaled = jnp.einsum("grt,gtd->grd", pick, near_upstream, preferred_element_type=f32)
    scaled = (scaled * gate_row).astype(bf16).reshape(grp, dev, SLOTS, feats)
    arrived, scaled = lax.optimization_barrier((arrived, scaled))
    scaled_rows = lax.all_to_all(scaled, "dev", split_axis=1, concat_axis=1, tiled=True)
    scaled_rows = scaled_rows.reshape(grp, dev * SLOTS, feats)
    arrived, scaled_rows = lax.optimization_barrier((arrived, scaled_rows))

    pre = lax.dot_general(
        w_all.reshape(split * 2 * hidden_part, split * feats),
        arrived,
        (((1,), (1,)), ((), ())),
        preferred_element_type=f32,
    ).reshape(split, 2, hidden_part, dev * SLOTS)
    hidden = (jax.nn.silu(pre[:, 0]) * pre[:, 1]).astype(bf16).reshape(split * hidden_part, dev * SLOTS)
    hidden_all = lax.all_gather(hidden, "split", axis=0, tiled=False)

    out = jnp.einsum("gfr,fd->grd", hidden_all, w_down[0], preferred_element_type=f32).astype(bf16)
    returned = lax.all_to_all(
        out.reshape(grp, dev, SLOTS, feats), "dev", split_axis=1, concat_axis=1, tiled=True
    ).reshape(grp, dev * SLOTS, feats)
    grad_block = sum(
        jnp.dot(hidden_all[g], scaled_rows[g], preferred_element_type=f32) for g in range(grp)
    )

    mixed = sum(
        jnp.einsum("grt,grd->gtd", piece, returned, preferred_element_type=f32)
        for piece in bf16_pieces(weight, 2)
    ).astype(bf16)
    mixed = lax.all_to_all(mixed, "grp", split_axis=0, concat_axis=0, tiled=True)
    mixed = jnp.sum(mixed.astype(f32), axis=0).astype(bf16)

    dots = jnp.einsum("grd,gtd->grt", returned, near_upstream, preferred_element_type=f32)
    dots = jnp.where(chosen, dots.reshape(grp, dev, SLOTS, rows), 0.0).sum(axis=2)
    grads = jnp.stack([jnp.sum(jnp.where(e, dots, 0.0), axis=1) for e in equal], axis=1)
    grads = jnp.broadcast_to(grads[:, None], (grp, split, top, rows)).reshape(grp * split, top, rows)
    grads = lax.all_to_all(grads, ("grp", "split"), split_axis=0, concat_axis=0, tiled=True)
    gate_grads = jnp.sum(grads, axis=0).T
    return (mixed, gate_grads, grad_block[None])


def solution(mesh):
    return jax.shard_map(
        per_device,
        mesh=mesh,
        in_specs=(
            P(("grp", "dev"), "split"),
            P(("grp", "dev"), "split"),
            P(("grp", "dev"), None),
            P(("grp", "dev"), None),
            P(("grp", "dev"), None, "split"),
            P(("grp", "dev"), None, "split"),
            P(("grp", "dev"), None, "split"),
        ),
        out_specs=(
            P(("grp", "dev"), "split"),
            P(("grp", "dev"), None),
            P(("grp", "dev"), None, "split"),
        ),
        check_vma=False,
    )
```

```python
import jax
import jax.numpy as jnp
from jax import lax
from jax.sharding import PartitionSpec as P

SLOTS = 16


def bf16_pieces(x, count):
    pieces = []
    for _ in range(count):
        top = lax.reduce_precision(x, exponent_bits=8, mantissa_bits=7)
        pieces.append(top.astype(jnp.bfloat16))
        x = x - top
    return pieces


def per_device(tokens, upstream, expert_ids, gate_probs, w_gate, w_up, w_down):
    grp = lax.axis_size("grp")
    dev = lax.axis_size("dev")
    split = lax.axis_size("split")
    grp_me = lax.axis_index("grp")
    split_me = lax.axis_index("split")
    rows, top = expert_ids.shape
    feats = tokens.shape[1]
    hidden_part = w_gate.shape[2]
    f32, bf16 = jnp.float32, jnp.bfloat16

    w_own = jnp.concatenate([w_gate[0].T, w_up[0].T], axis=0)
    w_all = lax.all_gather(w_own, "split", axis=0, tiled=False)

    def flipped(size, bits):
        return [(i, i ^ bits) for i in range(size)]

    def spread(x):
        x = jnp.broadcast_to(x[None], (grp,) + x.shape)
        return lax.all_to_all(x, "grp", split_axis=0, concat_axis=0, tiled=True)

    def relative(x):
        parts = [lax.dynamic_index_in_dim(x, split_me ^ j, 0, keepdims=True) for j in range(grp)]
        return jnp.concatenate(parts, axis=0)

    meta = jnp.concatenate([expert_ids.T.astype(bf16)] + bf16_pieces(gate_probs.T, 3), axis=0)
    meta = meta.reshape(-1, feats)
    meta_rows = meta.shape[0]
    meta = jnp.pad(meta, ((0, SLOTS - meta_rows), (0, 0)))
    near = spread(jnp.concatenate([upstream, meta], axis=0))
    near_meta = relative(near[:, rows : rows + meta_rows].reshape(grp, 4, top, rows).astype(f32))
    near_ids = near_meta[:, 0]
    near_gates = near_meta[:, 1] + near_meta[:, 2] + near_meta[:, 3]
    near_upstream = relative(near[:, :rows])

    near_tokens = jnp.stack(
        [tokens] + [lax.ppermute(tokens, "grp", flipped(grp, m)) for m in range(1, grp)]
    )
    mine = []
    for m in range(split):
        piece = lax.dynamic_index_in_dim(near_tokens, grp_me ^ split_me ^ m, 0, keepdims=False)
        mine.append(lax.ppermute(piece, "split", flipped(split, m)) if m > 0 else piece)
    mine = relative(jnp.stack(mine))
    mine = jnp.concatenate([mine[i] for i in range(split)], axis=1)

    expert = (grp_me * dev).astype(f32) + lax.broadcasted_iota(f32, (1, dev, 1), 1)
    equal = [near_ids[:, k][:, None, :] == expert for k in range(top)]
    member = sum(e.astype(f32) for e in equal)
    gate_of = sum(jnp.where(e, near_gates[:, k][:, None, :], 0.0) for k, e in enumerate(equal))
    before = (
        lax.broadcasted_iota(jnp.int32, (rows, rows), 0) < lax.broadcasted_iota(jnp.int32, (rows, rows), 1)
    ).astype(bf16)
    place = jnp.dot(member.astype(bf16).reshape(grp * dev, rows), before, preferred_element_type=f32)
    place = jnp.where(member > 0, place.reshape(grp, dev, rows), -1.0)
    slot = lax.broadcasted_iota(f32, (1, 1, SLOTS, 1), 2)
    chosen = place[:, :, None, :] == slot
    pick = chosen.astype(bf16).reshape(grp, dev * SLOTS, rows)
    weight = jnp.where(chosen, gate_of[:, :, None, :], 0.0).reshape(grp, dev * SLOTS, rows)
    gate_row = jnp.sum(weight, axis=2, keepdims=True)

    scaled = jnp.einsum("grt,gtd->grd", pick, near_upstream, preferred_element_type=f32)
    scaled = (scaled * gate_row).astype(bf16).reshape(grp, dev, SLOTS, feats)
    scaled_rows = lax.all_to_all(scaled, "dev", split_axis=1, concat_axis=1, tiled=True)
    scaled_rows = scaled_rows.reshape(grp, dev * SLOTS, feats)
    send = jnp.dot(pick[0], mine, preferred_element_type=f32).astype(bf16)
    send, scaled_rows = lax.optimization_barrier((send, scaled_rows))
    arrived = lax.all_to_all(
        send.reshape(dev, SLOTS, split * feats), "dev", split_axis=0, concat_axis=0, tiled=True
    ).reshape(dev * SLOTS, split * feats)

    pre = lax.dot_general(
        w_all.reshape(split * 2 * hidden_part, split * feats),
        arrived,
        (((1,), (1,)), ((), ())),
        preferred_element_type=f32,
    ).reshape(split, 2, hidden_part, dev * SLOTS)
    hidden = (jax.nn.silu(pre[:, 0]) * pre[:, 1]).astype(bf16).reshape(split * hidden_part, dev * SLOTS)
    hidden_of = [hidden]
    hidden_of.append(lax.ppermute(hidden, "split", flipped(split, 1)))
    hidden_of.append(lax.ppermute(hidden, "split", flipped(split, 2)))
    hidden_of[1:] = lax.optimization_barrier(tuple(hidden_of[1:]))
    hidden_of.append(lax.ppermute(hidden_of[2], "split", flipped(split, 1)))

    mixed, dots = [], []
    for j in range(0, grp, 2):
        two = slice(j, j + 2)
        out = jnp.stack(
            [
                lax.dot_general(h, w_down[0], (((0,), (0,)), ((), ())), preferred_element_type=f32).astype(bf16)
                for h in hidden_of[two]
            ]
        )
        returned = lax.all_to_all(
            out.reshape(2, dev, SLOTS, feats), "dev", split_axis=1, concat_axis=1, tiled=True
        ).reshape(2, dev * SLOTS, feats)
        mixed.append(
            sum(
                jnp.einsum("grt,grd->gtd", piece, returned, preferred_element_type=f32)
                for piece in bf16_pieces(weight[two], 2)
            ).astype(bf16)
        )
        part = jnp.einsum("grd,gtd->grt", returned, near_upstream[two], preferred_element_type=f32)
        dots.append(jnp.where(chosen[two], part.reshape(2, dev, SLOTS, rows), 0.0).sum(axis=2))
    mixed = jnp.concatenate(mixed, axis=0)
    dots = jnp.concatenate(dots, axis=0)
    grads = jnp.stack([jnp.sum(jnp.where(e, dots, 0.0), axis=1) for e in equal], axis=1)
    grads = relative(grads)
    grads = jnp.broadcast_to(grads[:, None], (grp, split, top, rows)).reshape(grp * split, top, rows)
    grads = lax.all_to_all(grads, ("grp", "split"), split_axis=0, concat_axis=0, tiled=True)
    gate_grads = jnp.sum(grads, axis=0).T

    total = 0.0
    for m in range(grp):
        piece = lax.dynamic_index_in_dim(mixed, grp_me ^ split_me ^ m, 0, keepdims=False)
        if m > 0:
            piece = lax.ppermute(piece, "grp", flipped(grp, m))
        total = total + piece.astype(f32)

    grad_block = sum(
        jnp.dot(hidden_of[j], scaled_rows[j], preferred_element_type=f32) for j in range(grp)
    )
    return (total.astype(bf16), gate_grads, grad_block[None])


def solution(mesh):
    return jax.shard_map(
        per_device,
        mesh=mesh,
        in_specs=(
            P(("grp", "dev"), "split"),
            P(("grp", "dev"), "split"),
            P(("grp", "dev"), None),
            P(("grp", "dev"), None),
            P(("grp", "dev"), None, "split"),
            P(("grp", "dev"), None, "split"),
            P(("grp", "dev"), None, "split"),
        ),
        out_specs=(
            P(("grp", "dev"), "split"),
            P(("grp", "dev"), None),
            P(("grp", "dev"), None, "split"),
        ),
        check_vma=False,
    )
```

```python
import jax
import jax.numpy as jnp
from jax import lax
from jax.sharding import PartitionSpec as P

SLOTS = 16


def bf16_pieces(x, count):
    pieces = []
    for _ in range(count):
        top = lax.reduce_precision(x, exponent_bits=8, mantissa_bits=7)
        pieces.append(top.astype(jnp.bfloat16))
        x = x - top
    return pieces


def per_device(tokens, upstream, expert_ids, gate_probs, w_gate, w_up, w_down):
    grp = lax.axis_size("grp")
    dev = lax.axis_size("dev")
    split = lax.axis_size("split")
    grp_me = lax.axis_index("grp")
    split_me = lax.axis_index("split")
    rows, top = expert_ids.shape
    feats = tokens.shape[1]
    hidden_part = w_gate.shape[2]
    f32, bf16 = jnp.float32, jnp.bfloat16

    def flipped(size, bits):
        return [(i, i ^ bits) for i in range(size)]

    def spread(x):
        x = jnp.broadcast_to(x[None], (grp,) + x.shape)
        return lax.all_to_all(x, "grp", split_axis=0, concat_axis=0, tiled=True)

    def relative(x):
        parts = [lax.dynamic_index_in_dim(x, split_me ^ j, 0, keepdims=True) for j in range(grp)]
        return jnp.concatenate(parts, axis=0)

    pieces = jnp.stack(
        [
            lax.ppermute(
                tokens,
                ("grp", "split"),
                [(g * split + f, (f ^ m) * split + g) for g in range(grp) for f in range(split)],
            )
            for m in range(split)
        ]
    )

    meta = jnp.concatenate([expert_ids.T.astype(bf16)] + bf16_pieces(gate_probs.T, 3), axis=0)
    meta = meta.reshape(-1, feats)
    meta_rows = meta.shape[0]
    meta = jnp.pad(meta, ((0, SLOTS - meta_rows), (0, 0)))
    near = spread(jnp.concatenate([upstream, meta], axis=0))
    w_own = jnp.concatenate([w_gate[0].T, w_up[0].T], axis=0)
    near, pieces, w_own = lax.optimization_barrier((near, pieces, w_own))

    w_all = lax.all_gather(w_own, "split", axis=0, tiled=False)

    near_meta = relative(near[:, rows : rows + meta_rows].reshape(grp, 4, top, rows).astype(f32))
    near_ids = near_meta[:, 0]
    near_gates = near_meta[:, 1] + near_meta[:, 2] + near_meta[:, 3]
    near_upstream = relative(near[:, :rows])

    mine = jnp.stack([lax.dynamic_index_in_dim(pieces, grp_me ^ f, 0, keepdims=False) for f in range(split)])
    mine = jnp.concatenate([mine[f] for f in range(split)], axis=1)

    expert = (grp_me * dev).astype(f32) + lax.broadcasted_iota(f32, (1, dev, 1), 1)
    equal = [near_ids[:, k][:, None, :] == expert for k in range(top)]
    member = sum(e.astype(f32) for e in equal)
    gate_of = sum(jnp.where(e, near_gates[:, k][:, None, :], 0.0) for k, e in enumerate(equal))
    before = (
        lax.broadcasted_iota(jnp.int32, (rows, rows), 0) < lax.broadcasted_iota(jnp.int32, (rows, rows), 1)
    ).astype(bf16)
    place = jnp.dot(member.astype(bf16).reshape(grp * dev, rows), before, preferred_element_type=f32)
    place = jnp.where(member > 0, place.reshape(grp, dev, rows), -1.0)
    slot = lax.broadcasted_iota(f32, (1, 1, SLOTS, 1), 2)
    chosen = place[:, :, None, :] == slot
    pick = chosen.astype(bf16).reshape(grp, dev * SLOTS, rows)
    weight = jnp.where(chosen, gate_of[:, :, None, :], 0.0).reshape(grp, dev * SLOTS, rows)
    gate_row = jnp.sum(weight, axis=2, keepdims=True)

    scaled = jnp.einsum("grt,gtd->grd", pick, near_upstream, preferred_element_type=f32)
    scaled = (scaled * gate_row).astype(bf16).reshape(grp, dev, SLOTS, feats)
    scaled_rows = lax.all_to_all(scaled, "dev", split_axis=1, concat_axis=1, tiled=True)
    scaled_rows = scaled_rows.reshape(grp, dev * SLOTS, feats)
    send = jnp.dot(pick[0], mine, preferred_element_type=f32).astype(bf16)
    send, scaled_rows = lax.optimization_barrier((send, scaled_rows))
    arrived = lax.all_to_all(
        send.reshape(dev, SLOTS, split * feats), "dev", split_axis=0, concat_axis=0, tiled=True
    ).reshape(dev * SLOTS, split * feats)

    pre = lax.dot_general(
        w_all.reshape(split * 2 * hidden_part, split * feats),
        arrived,
        (((1,), (1,)), ((), ())),
        preferred_element_type=f32,
    ).reshape(split, 2, hidden_part, dev * SLOTS)
    hidden = (jax.nn.silu(pre[:, 0]) * pre[:, 1]).astype(bf16).reshape(split * hidden_part, dev * SLOTS)
    hidden_of = [hidden]
    hidden_of.append(lax.ppermute(hidden, "split", flipped(split, 1)))
    hidden_of.append(lax.ppermute(hidden, "split", flipped(split, 2)))

    mixed, dots = [], []
    for part_of in (slice(0, 1), slice(1, 3), slice(3, 4)):
        count = part_of.stop - part_of.start
        if part_of.start == 1:
            returned, *hidden_of[1:] = lax.optimization_barrier((returned, *hidden_of[1:]))
            hidden_of.append(lax.ppermute(hidden_of[2], "split", flipped(split, 1)))
        if part_of.start == 3:
            returned, hidden_of[3] = lax.optimization_barrier((returned, hidden_of[3]))
        out = jnp.stack(
            [
                lax.dot_general(h, w_down[0], (((0,), (0,)), ((), ())), preferred_element_type=f32).astype(bf16)
                for h in hidden_of[part_of]
            ]
        )
        returned = lax.all_to_all(
            out.reshape(count, dev, SLOTS, feats), "dev", split_axis=1, concat_axis=1, tiled=True
        ).reshape(count, dev * SLOTS, feats)
        mixed.append(
            sum(
                jnp.einsum("grt,grd->gtd", piece, returned, preferred_element_type=f32)
                for piece in bf16_pieces(weight[part_of], 2)
            ).astype(bf16)
        )
        part = jnp.einsum("grd,gtd->grt", returned, near_upstream[part_of], preferred_element_type=f32)
        dots.append(jnp.where(chosen[part_of], part.reshape(count, dev, SLOTS, rows), 0.0).sum(axis=2))
    mixed = jnp.concatenate(mixed, axis=0)
    dots = jnp.concatenate(dots, axis=0)
    grads = jnp.stack([jnp.sum(jnp.where(e, dots, 0.0), axis=1) for e in equal], axis=1)
    grads = relative(grads)
    grads = jnp.broadcast_to(grads[:, None], (grp, split, top, rows)).reshape(grp * split, top, rows)
    grads = lax.all_to_all(grads, ("grp", "split"), split_axis=0, concat_axis=0, tiled=True)
    gate_grads = jnp.sum(grads, axis=0).T

    total = 0.0
    for m in range(grp):
        piece = lax.dynamic_index_in_dim(mixed, grp_me ^ split_me ^ m, 0, keepdims=False)
        if m > 0:
            piece = lax.ppermute(piece, "grp", flipped(grp, m))
        total = total + piece.astype(f32)

    grad_block = sum(
        jnp.dot(hidden_of[j], scaled_rows[j], preferred_element_type=f32) for j in range(grp)
    )
    return (total.astype(bf16), gate_grads, grad_block[None])


def solution(mesh):
    return jax.shard_map(
        per_device,
        mesh=mesh,
        in_specs=(
            P(("grp", "dev"), "split"),
            P(("grp", "dev"), "split"),
            P(("grp", "dev"), None),
            P(("grp", "dev"), None),
            P(("grp", "dev"), None, "split"),
            P(("grp", "dev"), None, "split"),
            P(("grp", "dev"), None, "split"),
        ),
        out_specs=(
            P(("grp", "dev"), "split"),
            P(("grp", "dev"), None),
            P(("grp", "dev"), None, "split"),
        ),
        check_vma=False,
    )
```

```python
import jax
import jax.numpy as jnp
from jax import lax
from jax.sharding import PartitionSpec as P

SLOTS = 16


def bf16_pieces(x, count):
    pieces = []
    for _ in range(count):
        top = lax.reduce_precision(x, exponent_bits=8, mantissa_bits=7)
        pieces.append(top.astype(jnp.bfloat16))
        x = x - top
    return pieces


def after(x, earlier):
    return x + (earlier[(0,) * earlier.ndim].astype(jnp.float32) * 0.0).astype(x.dtype)


def per_device(tokens, upstream, expert_ids, gate_probs, w_gate, w_up, w_down):
    grp = lax.axis_size("grp")
    dev = lax.axis_size("dev")
    split = lax.axis_size("split")
    grp_me = lax.axis_index("grp")
    split_me = lax.axis_index("split")
    rows, top = expert_ids.shape
    feats = tokens.shape[1]
    hidden_part = w_gate.shape[2]
    f32, bf16 = jnp.float32, jnp.bfloat16

    def flipped(size, bits):
        return [(i, i ^ bits) for i in range(size)]

    def spread(x):
        x = jnp.broadcast_to(x[None], (grp,) + x.shape)
        return lax.all_to_all(x, "grp", split_axis=0, concat_axis=0, tiled=True)

    def relative(x):
        parts = [lax.dynamic_index_in_dim(x, split_me ^ j, 0, keepdims=True) for j in range(grp)]
        return jnp.concatenate(parts, axis=0)

    pieces = jnp.stack(
        [
            lax.ppermute(
                tokens,
                ("grp", "split"),
                [(g * split + f, (f ^ m) * split + g) for g in range(grp) for f in range(split)],
            )
            for m in range(split)
        ]
    )

    meta = jnp.concatenate([expert_ids.T.astype(bf16)] + bf16_pieces(gate_probs.T, 3), axis=0)
    near = spread(meta)
    w_own = jnp.concatenate([w_gate[0].T, w_up[0].T], axis=0)
    w_own = after(after(w_own, near), pieces)

    w_of = [w_own]
    w_of.append(lax.ppermute(w_own, "split", flipped(split, 1)))
    w_of.append(lax.ppermute(w_own, "split", flipped(split, 2)))
    w_of[2] = after(w_of[2], w_of[1])
    w_of.append(lax.ppermute(w_of[2], "split", flipped(split, 1)))

    near_upstream = jnp.stack(
        [upstream] + [lax.ppermute(upstream, "grp", flipped(grp, m)) for m in range(1, grp)]
    )
    near_upstream = jnp.stack(
        [
            lax.dynamic_index_in_dim(near_upstream, grp_me ^ split_me ^ j, 0, keepdims=False)
            for j in range(grp)
        ]
    )

    near_meta = relative(near.astype(f32).reshape(grp, 4, top, rows))
    near_ids = near_meta[:, 0]
    near_gates = near_meta[:, 1] + near_meta[:, 2] + near_meta[:, 3]

    mine = jnp.stack([lax.dynamic_index_in_dim(pieces, grp_me ^ f, 0, keepdims=False) for f in range(split)])
    mine = jnp.concatenate([mine[f] for f in range(split)], axis=1)

    expert = (grp_me * dev).astype(f32) + lax.broadcasted_iota(f32, (1, dev, 1), 1)
    equal = [near_ids[:, k][:, None, :] == expert for k in range(top)]
    member = sum(e.astype(f32) for e in equal)
    gate_of = sum(jnp.where(e, near_gates[:, k][:, None, :], 0.0) for k, e in enumerate(equal))
    before = (
        lax.broadcasted_iota(jnp.int32, (rows, rows), 0) < lax.broadcasted_iota(jnp.int32, (rows, rows), 1)
    ).astype(bf16)
    place = jnp.dot(member.astype(bf16).reshape(grp * dev, rows), before, preferred_element_type=f32)
    place = jnp.where(member > 0, place.reshape(grp, dev, rows), -1.0)
    slot = lax.broadcasted_iota(f32, (1, 1, SLOTS, 1), 2)
    chosen = place[:, :, None, :] == slot
    pick = chosen.astype(bf16).reshape(grp, dev * SLOTS, rows)
    weight = jnp.where(chosen, gate_of[:, :, None, :], 0.0).reshape(grp, dev * SLOTS, rows)
    gate_row = jnp.sum(weight, axis=2, keepdims=True)

    send = jnp.dot(pick[0], mine, preferred_element_type=f32).astype(bf16)
    arrived = lax.all_to_all(
        send.reshape(dev, SLOTS, split * feats), "dev", split_axis=0, concat_axis=0, tiled=True
    ).reshape(dev * SLOTS, split * feats)
    scaled = jnp.einsum("grt,gtd->grd", pick, near_upstream, preferred_element_type=f32)
    scaled = (scaled * after(gate_row, arrived)).astype(bf16).reshape(grp, dev, SLOTS, feats)
    scaled_rows = lax.all_to_all(scaled, "dev", split_axis=1, concat_axis=1, tiled=True)
    scaled_rows = scaled_rows.reshape(grp, dev * SLOTS, feats)

    hidden = []
    for w in w_of:
        pre = lax.dot_general(w, arrived, (((1,), (1,)), ((), ())), preferred_element_type=f32)
        hidden.append((jax.nn.silu(pre[:hidden_part]) * pre[hidden_part:]).astype(bf16))
    hidden = relative(jnp.stack(hidden)).reshape(split * hidden_part, dev * SLOTS)
    hidden_of = [hidden]
    hidden_of.append(lax.ppermute(hidden, "split", flipped(split, 1)))
    hidden_of.append(lax.ppermute(hidden, "split", flipped(split, 2)))

    mixed, dots, returned = [], [], scaled_rows
    for part_of in (slice(0, 1), slice(1, 3), slice(3, 4)):
        count = part_of.stop - part_of.start
        if part_of.start == 1:
            hidden_of.append(lax.ppermute(hidden_of[2], "split", flipped(split, 1)))
        out = [
            lax.dot_general(h, w_down[0], (((0,), (0,)), ((), ())), preferred_element_type=f32)
            for h in hidden_of[part_of]
        ]
        out = jnp.stack([after(x, returned).astype(bf16) for x in out])
        returned = lax.all_to_all(
            out.reshape(count, dev, SLOTS, feats), "dev", split_axis=1, concat_axis=1, tiled=True
        ).reshape(count, dev * SLOTS, feats)
        mixed.append(
            sum(
                jnp.einsum("grt,grd->gtd", piece, returned, preferred_element_type=f32)
                for piece in bf16_pieces(weight[part_of], 2)
            ).astype(bf16)
        )
        part = jnp.einsum("grd,gtd->grt", returned, near_upstream[part_of], preferred_element_type=f32)
        dots.append(jnp.where(chosen[part_of], part.reshape(count, dev, SLOTS, rows), 0.0).sum(axis=2))
    mixed = jnp.concatenate(mixed, axis=0)
    dots = jnp.concatenate(dots, axis=0)
    grads = jnp.stack([jnp.sum(jnp.where(e, dots, 0.0), axis=1) for e in equal], axis=1)
    own_mixed = [
        lax.dynamic_index_in_dim(mixed, grp_me ^ split_me ^ m, 0, keepdims=False) for m in range(grp)
    ]
    grads = after(relative(grads), own_mixed[1])
    total = own_mixed[0].astype(f32)
    for m in range(1, grp):
        total = total + lax.ppermute(own_mixed[m], "grp", flipped(grp, m)).astype(f32)
    grads = jnp.broadcast_to(grads[:, None], (grp, split, top, rows)).reshape(grp * split, top, rows)
    grads = lax.all_to_all(grads, ("grp", "split"), split_axis=0, concat_axis=0, tiled=True)
    gate_grads = jnp.sum(grads, axis=0).T

    grad_block = sum(
        jnp.dot(hidden_of[j], scaled_rows[j], preferred_element_type=f32) for j in range(grp)
    )
    return (total.astype(bf16), gate_grads, grad_block[None])


def solution(mesh):
    return jax.shard_map(
        per_device,
        mesh=mesh,
        in_specs=(
            P(("grp", "dev"), "split"),
            P(("grp", "dev"), "split"),
            P(("grp", "dev"), None),
            P(("grp", "dev"), None),
            P(("grp", "dev"), None, "split"),
            P(("grp", "dev"), None, "split"),
            P(("grp", "dev"), None, "split"),
        ),
        out_specs=(
            P(("grp", "dev"), "split"),
            P(("grp", "dev"), None),
            P(("grp", "dev"), None, "split"),
        ),
        check_vma=False,
    )
```

```python
import jax
import jax.numpy as jnp
from jax import lax
from jax.sharding import PartitionSpec as P

SLOTS = 16


def bf16_pieces(x, count):
    pieces = []
    for _ in range(count):
        top = lax.reduce_precision(x, exponent_bits=8, mantissa_bits=7)
        pieces.append(top.astype(jnp.bfloat16))
        x = x - top
    return pieces


def after(x, earlier):
    return x + (earlier[(0,) * earlier.ndim].astype(jnp.float32) * 0.0).astype(x.dtype)


def per_device(tokens, upstream, expert_ids, gate_probs, w_gate, w_up, w_down):
    grp = lax.axis_size("grp")
    dev = lax.axis_size("dev")
    split = lax.axis_size("split")
    grp_me = lax.axis_index("grp")
    split_me = lax.axis_index("split")
    rows, top = expert_ids.shape
    feats = tokens.shape[1]
    hidden_part = w_gate.shape[2]
    f32, bf16 = jnp.float32, jnp.bfloat16

    def flipped(size, bits):
        return [(i, i ^ bits) for i in range(size)]

    def spread(x):
        x = jnp.broadcast_to(x[None], (grp,) + x.shape)
        return lax.all_to_all(x, "grp", split_axis=0, concat_axis=0, tiled=True)

    def relative(x):
        parts = [lax.dynamic_index_in_dim(x, split_me ^ j, 0, keepdims=True) for j in range(grp)]
        return jnp.concatenate(parts, axis=0)

    w_own = jnp.concatenate([w_gate[0].T, w_up[0].T], axis=0)
    w_all = lax.all_gather(w_own, "split", axis=0, tiled=False)

    pieces = jnp.stack(
        [
            lax.ppermute(
                tokens,
                ("grp", "split"),
                [(g * split + f, (f ^ m) * split + g) for g in range(grp) for f in range(split)],
            )
            for m in range(split)
        ]
    )

    meta = jnp.concatenate([expert_ids.T.astype(bf16)] + bf16_pieces(gate_probs.T, 3), axis=0)
    near = spread(meta)
    near_upstream = jnp.stack(
        [upstream] + [lax.ppermute(upstream, "grp", flipped(grp, m)) for m in range(1, grp)]
    )
    near_upstream = jnp.stack(
        [
            lax.dynamic_index_in_dim(near_upstream, grp_me ^ split_me ^ j, 0, keepdims=False)
            for j in range(grp)
        ]
    )

    near_meta = relative(near.astype(f32).reshape(grp, 4, top, rows))
    near_ids = near_meta[:, 0]
    near_gates = near_meta[:, 1] + near_meta[:, 2] + near_meta[:, 3]

    mine = jnp.stack([lax.dynamic_index_in_dim(pieces, grp_me ^ f, 0, keepdims=False) for f in range(split)])
    mine = jnp.concatenate([mine[f] for f in range(split)], axis=1)

    expert = (grp_me * dev).astype(f32) + lax.broadcasted_iota(f32, (1, dev, 1), 1)
    equal = [near_ids[:, k][:, None, :] == expert for k in range(top)]
    member = sum(e.astype(f32) for e in equal)
    gate_of = sum(jnp.where(e, near_gates[:, k][:, None, :], 0.0) for k, e in enumerate(equal))
    before = (
        lax.broadcasted_iota(jnp.int32, (rows, rows), 0) < lax.broadcasted_iota(jnp.int32, (rows, rows), 1)
    ).astype(bf16)
    place = jnp.dot(member.astype(bf16).reshape(grp * dev, rows), before, preferred_element_type=f32)
    place = jnp.where(member > 0, place.reshape(grp, dev, rows), -1.0)
    slot = lax.broadcasted_iota(f32, (1, 1, SLOTS, 1), 2)
    chosen = place[:, :, None, :] == slot
    pick = chosen.astype(bf16).reshape(grp, dev * SLOTS, rows)
    weight = jnp.where(chosen, gate_of[:, :, None, :], 0.0).reshape(grp, dev * SLOTS, rows)
    gate_row = jnp.sum(weight, axis=2, keepdims=True)

    send = jnp.dot(pick[0], mine, preferred_element_type=f32).astype(bf16)
    arrived = lax.all_to_all(
        send.reshape(dev, SLOTS, split * feats), "dev", split_axis=0, concat_axis=0, tiled=True
    ).reshape(dev * SLOTS, split * feats)
    scaled = jnp.einsum("grt,gtd->grd", pick, near_upstream, preferred_element_type=f32)
    scaled = (scaled * after(gate_row, arrived)).astype(bf16).reshape(grp, dev, SLOTS, feats)
    scaled_rows = lax.all_to_all(scaled, "dev", split_axis=1, concat_axis=1, tiled=True)
    scaled_rows = scaled_rows.reshape(grp, dev * SLOTS, feats)

    pre = lax.dot_general(
        w_all.reshape(split * 2 * hidden_part, split * feats),
        arrived,
        (((1,), (1,)), ((), ())),
        preferred_element_type=f32,
    ).reshape(split, 2, hidden_part, dev * SLOTS)
    hidden = (jax.nn.silu(pre[:, 0]) * pre[:, 1]).astype(bf16).reshape(split * hidden_part, dev * SLOTS)
    hidden_of = [hidden]
    hidden_of.append(lax.ppermute(hidden, "split", flipped(split, 1)))
    hidden_of.append(lax.ppermute(hidden, "split", flipped(split, 2)))

    mixed, dots, returned = [], [], scaled_rows
    for part_of in (slice(0, 1), slice(1, 3), slice(3, 4)):
        count = part_of.stop - part_of.start
        if part_of.start == 1:
            hidden_of.append(lax.ppermute(hidden_of[2], "split", flipped(split, 1)))
        out = [
            lax.dot_general(h, w_down[0], (((0,), (0,)), ((), ())), preferred_element_type=f32).astype(bf16)
            for h in hidden_of[part_of]
        ]
        out = after(lax.optimization_barrier(jnp.stack(out)), returned)
        returned = lax.all_to_all(
            out.reshape(count, dev, SLOTS, feats), "dev", split_axis=1, concat_axis=1, tiled=True
        ).reshape(count, dev * SLOTS, feats)
        mixed.append(
            sum(
                jnp.einsum("grt,grd->gtd", piece, returned, preferred_element_type=f32)
                for piece in bf16_pieces(weight[part_of], 2)
            ).astype(bf16)
        )
        part = jnp.einsum("grd,gtd->grt", returned, near_upstream[part_of], preferred_element_type=f32)
        dots.append(jnp.where(chosen[part_of], part.reshape(count, dev, SLOTS, rows), 0.0).sum(axis=2))
    mixed = jnp.concatenate(mixed, axis=0)
    dots = jnp.concatenate(dots, axis=0)
    grads = jnp.stack([jnp.sum(jnp.where(e, dots, 0.0), axis=1) for e in equal], axis=1)
    own_mixed = [
        lax.dynamic_index_in_dim(mixed, grp_me ^ split_me ^ m, 0, keepdims=False) for m in range(grp)
    ]
    grads = after(relative(grads), own_mixed[1])
    total = own_mixed[0].astype(f32)
    for m in range(1, grp):
        total = total + lax.ppermute(own_mixed[m], "grp", flipped(grp, m)).astype(f32)
    grads = jnp.broadcast_to(grads[:, None], (grp, split, top, rows)).reshape(grp * split, top, rows)
    grads = lax.all_to_all(grads, ("grp", "split"), split_axis=0, concat_axis=0, tiled=True)
    gate_grads = jnp.sum(grads, axis=0).T

    grad_block = sum(
        jnp.dot(hidden_of[j], scaled_rows[j], preferred_element_type=f32) for j in range(grp)
    )
    return (total.astype(bf16), gate_grads, grad_block[None])


def solution(mesh):
    return jax.shard_map(
        per_device,
        mesh=mesh,
        in_specs=(
            P(("grp", "dev"), "split"),
            P(("grp", "dev"), "split"),
            P(("grp", "dev"), None),
            P(("grp", "dev"), None),
            P(("grp", "dev"), None, "split"),
            P(("grp", "dev"), None, "split"),
            P(("grp", "dev"), None, "split"),
        ),
        out_specs=(
            P(("grp", "dev"), "split"),
            P(("grp", "dev"), None),
            P(("grp", "dev"), None, "split"),
        ),
        check_vma=False,
    )
```

```python
import jax
import jax.numpy as jnp
from jax import lax
from jax.experimental import pallas as pl
from jax.experimental.pallas import tpu as pltpu
from jax.sharding import PartitionSpec as P

SLOTS = 16


def bf16_pieces(x, count):
    pieces = []
    for _ in range(count):
        top = lax.reduce_precision(x, exponent_bits=8, mantissa_bits=7)
        pieces.append(top.astype(jnp.bfloat16))
        x = x - top
    return pieces


def after(x, earlier):
    return x + (earlier[(0,) * earlier.ndim].astype(jnp.float32) * 0.0).astype(x.dtype)


def expert_out(hidden_of, w_down, dev):
    count = len(hidden_of)
    hidden, feats = w_down.shape
    rows = hidden_of[0].shape[1]

    def kernel(*refs):
        w_ref, out_ref = refs[count], refs[-1]
        for c in range(count):
            rows_out = lax.dot_general(
                refs[c][...], w_ref[...], (((0,), (0,)), ((), ())), preferred_element_type=jnp.float32
            )
            out_ref[:, c] = rows_out.astype(jnp.bfloat16).reshape(dev, rows // dev, feats)

    vmem = pl.BlockSpec(memory_space=pltpu.VMEM)
    return pl.pallas_call(
        kernel,
        out_shape=jax.ShapeDtypeStruct((dev, count, rows // dev, feats), jnp.bfloat16),
        in_specs=[vmem] * (count + 1),
        out_specs=vmem,
        cost_estimate=pl.CostEstimate(
            flops=(1 if count == 1 else 32) * 2 * count * rows * hidden * feats,
            bytes_accessed=2 * (count * rows * (hidden + feats) + hidden * feats),
            transcendentals=0,
        ),
        compiler_params=pltpu.CompilerParams(vmem_limit_bytes=32 * 1024 * 1024),
    )(*hidden_of, w_down)


def per_device(tokens, upstream, expert_ids, gate_probs, w_gate, w_up, w_down):
    grp = lax.axis_size("grp")
    dev = lax.axis_size("dev")
    split = lax.axis_size("split")
    grp_me = lax.axis_index("grp")
    split_me = lax.axis_index("split")
    rows, top = expert_ids.shape
    feats = tokens.shape[1]
    hidden_part = w_gate.shape[2]
    f32, bf16 = jnp.float32, jnp.bfloat16

    def flipped(size, bits):
        return [(i, i ^ bits) for i in range(size)]

    def relative(x):
        parts = [lax.dynamic_index_in_dim(x, split_me ^ j, 0, keepdims=True) for j in range(grp)]
        return jnp.concatenate(parts, axis=0)

    w_own = jnp.concatenate([w_gate[0].T, w_up[0].T], axis=0)
    w_all = lax.all_gather(w_own, "split", axis=0, tiled=False)

    meta = jnp.concatenate([expert_ids.T.astype(bf16)] + bf16_pieces(gate_probs.T, 3), axis=0)
    meta = meta.reshape(-1, feats)
    meta_rows = meta.shape[0]
    meta = jnp.pad(meta, ((0, SLOTS - meta_rows), (0, 0)))
    token_rows = jnp.concatenate([tokens, meta], axis=0)
    upstream_rows = jnp.concatenate([upstream, meta], axis=0)

    pieces = jnp.stack(
        [
            lax.ppermute(
                token_rows,
                ("grp", "split"),
                [(g * split + f, (f ^ m) * split + g) for g in range(grp) for f in range(split)],
            )
            for m in range(split)
        ]
    )
    mine = [lax.dynamic_index_in_dim(pieces[:, :rows], grp_me ^ f, 0, keepdims=False) for f in range(split)]
    mine = jnp.concatenate(mine, axis=1)

    near = jnp.stack(
        [upstream_rows] + [lax.ppermute(upstream_rows, "grp", flipped(grp, m)) for m in range(1, grp)]
    )
    near = jnp.stack(
        [lax.dynamic_index_in_dim(near, grp_me ^ split_me ^ j, 0, keepdims=False) for j in range(grp)]
    )
    near_upstream = near[:, :rows]

    expert = (grp_me * dev).astype(f32) + lax.broadcasted_iota(f32, (1, dev, 1), 1)
    before = (
        lax.broadcasted_iota(jnp.int32, (rows, rows), 0) < lax.broadcasted_iota(jnp.int32, (rows, rows), 1)
    ).astype(bf16)
    slot = lax.broadcasted_iota(f32, (1, 1, SLOTS, 1), 2)

    def route(meta):
        count = meta.shape[0]
        meta = meta.astype(f32).reshape(count, 4, top, rows)
        equal = [meta[:, 0, k][:, None, :] == expert for k in range(top)]
        member = sum(e.astype(f32) for e in equal)
        place = jnp.dot(member.astype(bf16).reshape(count * dev, rows), before, preferred_element_type=f32)
        place = jnp.where(member > 0, place.reshape(count, dev, rows), -1.0)
        gates = meta[:, 1] + meta[:, 2] + meta[:, 3]
        return equal, gates, place[:, :, None, :] == slot

    _, _, chosen_mine = route(pieces[:1, rows : rows + meta_rows])
    equal, near_gates, chosen = route(near[:, rows : rows + meta_rows])
    gate_of = sum(jnp.where(e, near_gates[:, k][:, None, :], 0.0) for k, e in enumerate(equal))
    pick = chosen.astype(bf16).reshape(grp, dev * SLOTS, rows)
    weight = jnp.where(chosen, gate_of[:, :, None, :], 0.0).reshape(grp, dev * SLOTS, rows)
    gate_row = jnp.sum(weight, axis=2, keepdims=True)

    pick_mine = chosen_mine.astype(bf16).reshape(dev * SLOTS, rows)
    send = jnp.dot(pick_mine, mine, preferred_element_type=f32).astype(bf16)
    arrived = lax.all_to_all(
        send.reshape(dev, SLOTS, split * feats), "dev", split_axis=0, concat_axis=0, tiled=True
    ).reshape(dev * SLOTS, split * feats)
    scaled = jnp.einsum("grt,gtd->grd", pick, near_upstream, preferred_element_type=f32)
    scaled = (scaled * after(gate_row, arrived)).astype(bf16).reshape(grp, dev, SLOTS, feats)
    scaled_rows = lax.all_to_all(scaled, "dev", split_axis=1, concat_axis=1, tiled=True)
    scaled_rows = scaled_rows.reshape(grp, dev * SLOTS, feats)

    pre = lax.dot_general(
        w_all.reshape(split * 2 * hidden_part, split * feats),
        arrived,
        (((1,), (1,)), ((), ())),
        preferred_element_type=f32,
    ).reshape(split, 2, hidden_part, dev * SLOTS)
    hidden = (jax.nn.silu(pre[:, 0]) * pre[:, 1]).astype(bf16).reshape(split * hidden_part, dev * SLOTS)
    hidden_of = [hidden]
    hidden_of.append(lax.ppermute(hidden, "split", flipped(split, 1)))
    hidden_of.append(lax.ppermute(hidden, "split", flipped(split, 2)))

    mixed, dots, returned = [], [], scaled_rows
    for part_of in (slice(0, 1), slice(1, 3), slice(3, 4)):
        count = part_of.stop - part_of.start
        if part_of.start == 1:
            hidden_of.append(lax.ppermute(hidden_of[2], "split", flipped(split, 1)))
        out = after(expert_out(hidden_of[part_of], w_down[0], dev), returned)
        returned = lax.all_to_all(out, "dev", split_axis=0, concat_axis=0, tiled=True)
        sent = jnp.swapaxes(returned, 0, 1).reshape(count, dev * SLOTS, feats)
        mixed.append(
            sum(
                jnp.einsum("grt,grd->gtd", piece, sent, preferred_element_type=f32)
                for piece in bf16_pieces(weight[part_of], 2)
            ).astype(bf16)
        )
        part = jnp.einsum("grd,gtd->grt", sent, near_upstream[part_of], preferred_element_type=f32)
        dots.append(jnp.where(chosen[part_of], part.reshape(count, dev, SLOTS, rows), 0.0).sum(axis=2))
    mixed = jnp.concatenate(mixed, axis=0)
    dots = jnp.concatenate(dots, axis=0)
    grads = jnp.stack([jnp.sum(jnp.where(e, dots, 0.0), axis=1) for e in equal], axis=1)
    own_mixed = [
        lax.dynamic_index_in_dim(mixed, grp_me ^ split_me ^ m, 0, keepdims=False) for m in range(grp)
    ]
    grads = after(relative(grads), own_mixed[1])
    total = own_mixed[0].astype(f32)
    for m in range(1, grp):
        total = total + lax.ppermute(own_mixed[m], "grp", flipped(grp, m)).astype(f32)
    grads = jnp.broadcast_to(grads[:, None], (grp, split, top, rows)).reshape(grp * split, top, rows)
    grads = lax.all_to_all(grads, ("grp", "split"), split_axis=0, concat_axis=0, tiled=True)
    gate_grads = jnp.sum(grads, axis=0).T

    grad_block = sum(
        jnp.dot(hidden_of[j], scaled_rows[j], preferred_element_type=f32) for j in range(grp)
    )
    return (total.astype(bf16), gate_grads, grad_block[None])


def solution(mesh):
    return jax.shard_map(
        per_device,
        mesh=mesh,
        in_specs=(
            P(("grp", "dev"), "split"),
            P(("grp", "dev"), "split"),
            P(("grp", "dev"), None),
            P(("grp", "dev"), None),
            P(("grp", "dev"), None, "split"),
            P(("grp", "dev"), None, "split"),
            P(("grp", "dev"), None, "split"),
        ),
        out_specs=(
            P(("grp", "dev"), "split"),
            P(("grp", "dev"), None),
            P(("grp", "dev"), None, "split"),
        ),
        check_vma=False,
    )
```

```python
import jax
import jax.numpy as jnp
from jax import lax
from jax.experimental import pallas as pl
from jax.experimental.pallas import tpu as pltpu
from jax.sharding import PartitionSpec as P

SLOTS = 16


def bf16_pieces(x, count):
    pieces = []
    for _ in range(count):
        top = lax.reduce_precision(x, exponent_bits=8, mantissa_bits=7)
        pieces.append(top.astype(jnp.bfloat16))
        x = x - top
    return pieces


def after(x, earlier):
    return x + (earlier[(0,) * earlier.ndim].astype(jnp.float32) * 0.0).astype(x.dtype)


def expert_out(hidden_of, w_down, dev):
    count = len(hidden_of)
    hidden, feats = w_down.shape
    rows = hidden_of[0].shape[1]

    def kernel(*refs):
        w_ref, out_ref = refs[count], refs[-1]
        for c in range(count):
            rows_out = lax.dot_general(
                refs[c][...], w_ref[...], (((0,), (0,)), ((), ())), preferred_element_type=jnp.float32
            )
            out_ref[:, c] = rows_out.astype(jnp.bfloat16).reshape(dev, rows // dev, feats)

    vmem = pl.BlockSpec(memory_space=pltpu.VMEM)
    return pl.pallas_call(
        kernel,
        out_shape=jax.ShapeDtypeStruct((dev, count, rows // dev, feats), jnp.bfloat16),
        in_specs=[vmem] * (count + 1),
        out_specs=vmem,
        cost_estimate=pl.CostEstimate(
            flops=(1 if count == 1 else 32) * 2 * count * rows * hidden * feats,
            bytes_accessed=2 * (count * rows * (hidden + feats) + hidden * feats),
            transcendentals=0,
        ),
        compiler_params=pltpu.CompilerParams(vmem_limit_bytes=32 * 1024 * 1024),
    )(*hidden_of, w_down)


def per_device(tokens, upstream, expert_ids, gate_probs, w_gate, w_up, w_down):
    grp = lax.axis_size("grp")
    dev = lax.axis_size("dev")
    split = lax.axis_size("split")
    grp_me = lax.axis_index("grp")
    split_me = lax.axis_index("split")
    rows, top = expert_ids.shape
    feats = tokens.shape[1]
    hidden_part = w_gate.shape[2]
    f32, bf16 = jnp.float32, jnp.bfloat16

    def flipped(size, bits):
        return [(i, i ^ bits) for i in range(size)]

    def relative(x):
        parts = [lax.dynamic_index_in_dim(x, split_me ^ j, 0, keepdims=True) for j in range(grp)]
        return jnp.concatenate(parts, axis=0)

    w_own = jnp.concatenate([w_gate[0].T, w_up[0].T], axis=0)
    w_all = lax.all_gather(w_own, "split", axis=0, tiled=False)

    meta = jnp.concatenate([expert_ids.T.astype(bf16)] + bf16_pieces(gate_probs.T, 3), axis=0)
    meta = meta.reshape(-1, feats)
    meta_rows = meta.shape[0]
    meta = jnp.pad(meta, ((0, SLOTS - meta_rows), (0, 0)))
    token_rows = jnp.concatenate([tokens, meta], axis=0)
    upstream_rows = jnp.concatenate([upstream, meta], axis=0)

    core = flipped(grp, 1)
    pieces = [None] * split
    for m in (0, 2):
        pieces[m] = lax.ppermute(
            token_rows,
            ("grp", "split"),
            [(g * split + f, (f ^ m) * split + g) for g in range(grp) for f in range(split)],
        )
        pieces[m + 1] = lax.ppermute(pieces[m], "grp", core)
    pieces = jnp.stack(pieces)
    mine = [lax.dynamic_index_in_dim(pieces[:, :rows], grp_me ^ f, 0, keepdims=False) for f in range(split)]
    mine = jnp.concatenate(mine, axis=1)

    far = lax.ppermute(upstream_rows, "grp", flipped(grp, 2))
    near = jnp.stack(
        [upstream_rows, lax.ppermute(upstream_rows, "grp", core), far, lax.ppermute(far, "grp", core)]
    )
    near = jnp.stack(
        [lax.dynamic_index_in_dim(near, grp_me ^ split_me ^ j, 0, keepdims=False) for j in range(grp)]
    )
    near_upstream = near[:, :rows]

    expert = (grp_me * dev).astype(f32) + lax.broadcasted_iota(f32, (1, dev, 1), 1)
    before = (
        lax.broadcasted_iota(jnp.int32, (rows, rows), 0) < lax.broadcasted_iota(jnp.int32, (rows, rows), 1)
    ).astype(bf16)
    slot = lax.broadcasted_iota(f32, (1, 1, SLOTS, 1), 2)

    def route(meta):
        count = meta.shape[0]
        meta = meta.astype(f32).reshape(count, 4, top, rows)
        equal = [meta[:, 0, k][:, None, :] == expert for k in range(top)]
        member = sum(e.astype(f32) for e in equal)
        place = jnp.dot(member.astype(bf16).reshape(count * dev, rows), before, preferred_element_type=f32)
        place = jnp.where(member > 0, place.reshape(count, dev, rows), -1.0)
        gates = meta[:, 1] + meta[:, 2] + meta[:, 3]
        return equal, gates, place[:, :, None, :] == slot

    _, _, chosen_mine = route(pieces[:1, rows : rows + meta_rows])
    equal, near_gates, chosen = route(near[:, rows : rows + meta_rows])
    gate_of = sum(jnp.where(e, near_gates[:, k][:, None, :], 0.0) for k, e in enumerate(equal))
    pick = chosen.astype(bf16).reshape(grp, dev * SLOTS, rows)
    weight = jnp.where(chosen, gate_of[:, :, None, :], 0.0).reshape(grp, dev * SLOTS, rows)
    gate_row = jnp.sum(weight, axis=2, keepdims=True)

    pick_mine = chosen_mine.astype(bf16).reshape(dev * SLOTS, rows)
    send = jnp.dot(pick_mine, mine, preferred_element_type=f32).astype(bf16)
    arrived = lax.all_to_all(
        send.reshape(dev, SLOTS, split * feats), "dev", split_axis=0, concat_axis=0, tiled=True
    ).reshape(dev * SLOTS, split * feats)
    scaled = jnp.einsum("grt,gtd->grd", pick, near_upstream, preferred_element_type=f32)
    scaled = (scaled * after(gate_row, arrived)).astype(bf16).reshape(grp, dev, SLOTS, feats)
    scaled_rows = lax.all_to_all(scaled, "dev", split_axis=1, concat_axis=1, tiled=True)
    scaled_rows = scaled_rows.reshape(grp, dev * SLOTS, feats)

    pre = lax.dot_general(
        w_all.reshape(split * 2 * hidden_part, split * feats),
        arrived,
        (((1,), (1,)), ((), ())),
        preferred_element_type=f32,
    ).reshape(split, 2, hidden_part, dev * SLOTS)
    hidden = (jax.nn.silu(pre[:, 0]) * pre[:, 1]).astype(bf16).reshape(split * hidden_part, dev * SLOTS)
    hidden_of = [hidden]
    hidden_of.append(lax.ppermute(hidden, "split", flipped(split, 1)))
    hidden_of.append(lax.ppermute(hidden, "split", flipped(split, 2)))

    mixed, dots, returned = [], [], scaled_rows
    for part_of in (slice(0, 1), slice(1, 3), slice(3, 4)):
        count = part_of.stop - part_of.start
        if part_of.start == 1:
            hidden_of.append(lax.ppermute(hidden_of[2], "split", flipped(split, 1)))
        out = after(expert_out(hidden_of[part_of], w_down[0], dev), returned)
        returned = lax.all_to_all(out, "dev", split_axis=0, concat_axis=0, tiled=True)
        sent = jnp.swapaxes(returned, 0, 1).reshape(count, dev * SLOTS, feats)
        mixed.append(
            sum(
                jnp.einsum("grt,grd->gtd", piece, sent, preferred_element_type=f32)
                for piece in bf16_pieces(weight[part_of], 2)
            ).astype(bf16)
        )
        part = jnp.einsum("grd,gtd->grt", sent, near_upstream[part_of], preferred_element_type=f32)
        dots.append(jnp.where(chosen[part_of], part.reshape(count, dev, SLOTS, rows), 0.0).sum(axis=2))
    mixed = jnp.concatenate(mixed, axis=0)
    dots = jnp.concatenate(dots, axis=0)
    grads = jnp.stack([jnp.sum(jnp.where(e, dots, 0.0), axis=1) for e in equal], axis=1)
    own_mixed = [
        lax.dynamic_index_in_dim(mixed, grp_me ^ split_me ^ m, 0, keepdims=False) for m in range(grp)
    ]
    grads = after(relative(grads), own_mixed[1])
    other = lax.ppermute(jnp.stack([own_mixed[1], own_mixed[3]]), "grp", core).astype(f32)
    far_sum = (own_mixed[2].astype(f32) + other[1]).astype(bf16)
    total = own_mixed[0].astype(f32) + other[0]
    total = total + lax.ppermute(far_sum, "grp", flipped(grp, 2)).astype(f32)
    grads = jnp.broadcast_to(grads[:, None], (grp, split, top, rows)).reshape(grp * split, top, rows)
    grads = lax.all_to_all(grads, ("grp", "split"), split_axis=0, concat_axis=0, tiled=True)
    gate_grads = jnp.sum(grads, axis=0).T

    grad_block = sum(
        jnp.dot(hidden_of[j], scaled_rows[j], preferred_element_type=f32) for j in range(grp)
    )
    return (total.astype(bf16), gate_grads, grad_block[None])


def solution(mesh):
    return jax.shard_map(
        per_device,
        mesh=mesh,
        in_specs=(
            P(("grp", "dev"), "split"),
            P(("grp", "dev"), "split"),
            P(("grp", "dev"), None),
            P(("grp", "dev"), None),
            P(("grp", "dev"), None, "split"),
            P(("grp", "dev"), None, "split"),
            P(("grp", "dev"), None, "split"),
        ),
        out_specs=(
            P(("grp", "dev"), "split"),
            P(("grp", "dev"), None),
            P(("grp", "dev"), None, "split"),
        ),
        check_vma=False,
    )
```

```python
import jax
import jax.numpy as jnp
from jax import lax
from jax.experimental import pallas as pl
from jax.experimental.pallas import tpu as pltpu
from jax.sharding import PartitionSpec as P

SLOTS = 16


def bf16_pieces(x, count):
    pieces = []
    for _ in range(count):
        top = lax.reduce_precision(x, exponent_bits=8, mantissa_bits=7)
        pieces.append(top.astype(jnp.bfloat16))
        x = x - top
    return pieces


def after(x, earlier):
    return x + (earlier[(0,) * earlier.ndim].astype(jnp.float32) * 0.0).astype(x.dtype)


def held(x, earlier):
    def kernel(x_ref, earlier_ref, out_ref):
        del x_ref, earlier_ref, out_ref

    anywhere = pl.BlockSpec(memory_space=pl.ANY)
    return pl.pallas_call(
        kernel,
        out_shape=jax.ShapeDtypeStruct(x.shape, x.dtype),
        in_specs=[anywhere, anywhere],
        out_specs=anywhere,
        input_output_aliases={0: 0},
        cost_estimate=pl.CostEstimate(flops=0, bytes_accessed=0, transcendentals=0),
    )(x, earlier)


def hidden_units(w_all, arrived):
    parts, both, width = w_all.shape
    half = both // 2
    rows = arrived.shape[0]

    def kernel(w_ref, x_ref, out_ref):
        pre = lax.dot_general(
            w_ref[0], x_ref[...], (((1,), (1,)), ((), ())), preferred_element_type=jnp.float32
        )
        gate, up = pre[:half], pre[half:]
        out_ref[...] = (gate / (1.0 + jnp.exp(-gate)) * up).astype(jnp.bfloat16)

    return pl.pallas_call(
        kernel,
        grid=(parts,),
        out_shape=jax.ShapeDtypeStruct((parts * half, rows), jnp.bfloat16),
        in_specs=[
            pl.BlockSpec((1, both, width), lambda q: (q, 0, 0)),
            pl.BlockSpec((rows, width), lambda q: (0, 0)),
        ],
        out_specs=pl.BlockSpec((half, rows), lambda q: (q, 0)),
        cost_estimate=pl.CostEstimate(
            flops=2 * parts * both * width * rows,
            bytes_accessed=2 * (parts * both * width + rows * width + parts * half * rows),
            transcendentals=parts * half * rows,
        ),
        compiler_params=pltpu.CompilerParams(vmem_limit_bytes=32 * 1024 * 1024),
    )(w_all, arrived)


def expert_out(hidden_of, w_down, dev):
    count = len(hidden_of)
    hidden, feats = w_down.shape
    rows = hidden_of[0].shape[1]

    def kernel(*refs):
        w_ref, out_ref = refs[count], refs[-1]
        for c in range(count):
            rows_out = lax.dot_general(
                refs[c][...], w_ref[...], (((0,), (0,)), ((), ())), preferred_element_type=jnp.float32
            )
            out_ref[:, c] = rows_out.astype(jnp.bfloat16).reshape(dev, rows // dev, feats)

    vmem = pl.BlockSpec(memory_space=pltpu.VMEM)
    return pl.pallas_call(
        kernel,
        out_shape=jax.ShapeDtypeStruct((dev, count, rows // dev, feats), jnp.bfloat16),
        in_specs=[vmem] * (count + 1),
        out_specs=vmem,
        cost_estimate=pl.CostEstimate(
            flops=(1 if count == 1 else 32) * 2 * count * rows * hidden * feats,
            bytes_accessed=2 * (count * rows * (hidden + feats) + hidden * feats),
            transcendentals=0,
        ),
        compiler_params=pltpu.CompilerParams(vmem_limit_bytes=32 * 1024 * 1024),
    )(*hidden_of, w_down)


def per_device(tokens, upstream, expert_ids, gate_probs, w_gate, w_up, w_down):
    grp = lax.axis_size("grp")
    dev = lax.axis_size("dev")
    split = lax.axis_size("split")
    grp_me = lax.axis_index("grp")
    split_me = lax.axis_index("split")
    rows, top = expert_ids.shape
    feats = tokens.shape[1]
    hidden_part = w_gate.shape[2]
    f32, bf16 = jnp.float32, jnp.bfloat16

    def flipped(size, bits):
        return [(i, i ^ bits) for i in range(size)]

    def relative(x):
        parts = [lax.dynamic_index_in_dim(x, split_me ^ j, 0, keepdims=True) for j in range(grp)]
        return jnp.concatenate(parts, axis=0)

    w_own = jnp.concatenate([w_gate[0].T, w_up[0].T], axis=0)
    w_all = lax.all_gather(w_own, "split", axis=0, tiled=False)

    meta = jnp.concatenate([expert_ids.T.astype(bf16)] + bf16_pieces(gate_probs.T, 3), axis=0)
    meta = meta.reshape(-1, feats)
    meta_rows = meta.shape[0]
    meta = jnp.pad(meta, ((0, SLOTS - meta_rows), (0, 0)))
    token_rows = jnp.concatenate([tokens, meta], axis=0)
    upstream_rows = jnp.concatenate([upstream, meta], axis=0)

    core = flipped(grp, 1)
    pieces = [None] * split
    for m in (0, 2):
        pieces[m] = lax.ppermute(
            token_rows,
            ("grp", "split"),
            [(g * split + f, (f ^ m) * split + g) for g in range(grp) for f in range(split)],
        )
        pieces[m + 1] = lax.ppermute(pieces[m], "grp", core)
    pieces = jnp.stack(pieces)
    mine = [lax.dynamic_index_in_dim(pieces[:, :rows], grp_me ^ f, 0, keepdims=False) for f in range(split)]
    mine = jnp.concatenate(mine, axis=1)

    far = lax.ppermute(upstream_rows, "grp", flipped(grp, 2))
    near = jnp.stack(
        [upstream_rows, lax.ppermute(upstream_rows, "grp", core), far, lax.ppermute(far, "grp", core)]
    )
    near = jnp.stack(
        [lax.dynamic_index_in_dim(near, grp_me ^ split_me ^ j, 0, keepdims=False) for j in range(grp)]
    )
    near_upstream = near[:, :rows]

    expert = (grp_me * dev).astype(f32) + lax.broadcasted_iota(f32, (1, dev, 1), 1)
    before = (
        lax.broadcasted_iota(jnp.int32, (rows, rows), 0) < lax.broadcasted_iota(jnp.int32, (rows, rows), 1)
    ).astype(bf16)
    slot = lax.broadcasted_iota(f32, (1, 1, SLOTS, 1), 2)

    def route(meta):
        count = meta.shape[0]
        meta = meta.astype(f32).reshape(count, 4, top, rows)
        equal = [meta[:, 0, k][:, None, :] == expert for k in range(top)]
        member = sum(e.astype(f32) for e in equal)
        place = jnp.dot(member.astype(bf16).reshape(count * dev, rows), before, preferred_element_type=f32)
        place = jnp.where(member > 0, place.reshape(count, dev, rows), -1.0)
        gates = meta[:, 1] + meta[:, 2] + meta[:, 3]
        return equal, gates, place[:, :, None, :] == slot

    _, _, chosen_mine = route(pieces[:1, rows : rows + meta_rows])
    equal, near_gates, chosen = route(near[:, rows : rows + meta_rows])
    gate_of = sum(jnp.where(e, near_gates[:, k][:, None, :], 0.0) for k, e in enumerate(equal))
    pick = chosen.astype(bf16).reshape(grp, dev * SLOTS, rows)
    weight = jnp.where(chosen, gate_of[:, :, None, :], 0.0).reshape(grp, dev * SLOTS, rows)
    gate_row = jnp.sum(weight, axis=2, keepdims=True)

    pick_mine = chosen_mine.astype(bf16).reshape(dev * SLOTS, rows)
    send = jnp.dot(pick_mine, mine, preferred_element_type=f32).astype(bf16)
    arrived = lax.all_to_all(
        send.reshape(dev, SLOTS, split * feats), "dev", split_axis=0, concat_axis=0, tiled=True
    ).reshape(dev * SLOTS, split * feats)
    scaled = jnp.einsum("grt,gtd->grd", pick, near_upstream, preferred_element_type=f32)
    scaled = (scaled * after(gate_row, arrived)).astype(bf16).reshape(grp, dev, SLOTS, feats)
    scaled_rows = lax.all_to_all(scaled, "dev", split_axis=1, concat_axis=1, tiled=True)
    scaled_rows = scaled_rows.reshape(grp, dev * SLOTS, feats)

    hidden = hidden_units(w_all, arrived)
    hidden_of = [hidden]
    hidden_of.append(lax.ppermute(hidden, "split", flipped(split, 1)))
    hidden_of.append(lax.ppermute(hidden, "split", flipped(split, 2)))

    mixed, dots, returned = [], [], scaled_rows
    for part_of in (slice(0, 1), slice(1, 3), slice(3, 4)):
        count = part_of.stop - part_of.start
        if part_of.start == 1:
            hidden_of.append(lax.ppermute(hidden_of[2], "split", flipped(split, 1)))
        out = held(expert_out(hidden_of[part_of], w_down[0], dev), returned)
        returned = lax.all_to_all(out, "dev", split_axis=0, concat_axis=0, tiled=True)
        sent = jnp.swapaxes(returned, 0, 1).reshape(count, dev * SLOTS, feats)
        mixed.append(
            sum(
                jnp.einsum("grt,grd->gtd", piece, sent, preferred_element_type=f32)
                for piece in bf16_pieces(weight[part_of], 2)
            ).astype(bf16)
        )
        part = jnp.einsum("grd,gtd->grt", sent, near_upstream[part_of], preferred_element_type=f32)
        dots.append(jnp.where(chosen[part_of], part.reshape(count, dev, SLOTS, rows), 0.0).sum(axis=2))
    mixed = jnp.concatenate(mixed, axis=0)
    dots = jnp.concatenate(dots, axis=0)
    grads = jnp.stack([jnp.sum(jnp.where(e, dots, 0.0), axis=1) for e in equal], axis=1)
    own_mixed = [
        lax.dynamic_index_in_dim(mixed, grp_me ^ split_me ^ m, 0, keepdims=False) for m in range(grp)
    ]
    grads = after(relative(grads), own_mixed[1])
    other = lax.ppermute(jnp.stack([own_mixed[1], own_mixed[3]]), "grp", core).astype(f32)
    far_sum = (own_mixed[2].astype(f32) + other[1]).astype(bf16)
    total = own_mixed[0].astype(f32) + other[0]
    total = total + lax.ppermute(far_sum, "grp", flipped(grp, 2)).astype(f32)
    grads = jnp.broadcast_to(grads[:, None], (grp, split, top, rows)).reshape(grp * split, top, rows)
    grads = lax.all_to_all(grads, ("grp", "split"), split_axis=0, concat_axis=0, tiled=True)
    gate_grads = jnp.sum(grads, axis=0).T

    grad_block = sum(
        jnp.dot(hidden_of[j], scaled_rows[j], preferred_element_type=f32) for j in range(grp)
    )
    return (total.astype(bf16), gate_grads, grad_block[None])


def solution(mesh):
    return jax.shard_map(
        per_device,
        mesh=mesh,
        in_specs=(
            P(("grp", "dev"), "split"),
            P(("grp", "dev"), "split"),
            P(("grp", "dev"), None),
            P(("grp", "dev"), None),
            P(("grp", "dev"), None, "split"),
            P(("grp", "dev"), None, "split"),
            P(("grp", "dev"), None, "split"),
        ),
        out_specs=(
            P(("grp", "dev"), "split"),
            P(("grp", "dev"), None),
            P(("grp", "dev"), None, "split"),
        ),
        check_vma=False,
    )
```
